32 devices in a mesh: chan: 4 (over z), bin: 8 (over y, x, core).
Axes of the slice: x: 2, y: 2, z: 4, core: 2. Of those that a mesh axis runs over, the one named last changes fastest.
Arguments:
- spectra: bfloat16 [64, 2, 512, 1024], P('bin', None, None, 'chan')
- valid: int32 [8, 512], P('chan'), may hold values from 0 to 1, as said below
Outputs:
- stacked: bfloat16 [8, 5, 64, 2, 128, 128], P('chan', None, 'bin')
The draws below stay inside these ranges and needn't reach their ends.
Inputs may be any that keep to these rules, and one draw needn't show every extreme that they name: `valid`: each entry is 0 or 1; in every draw exactly one channel block, drawn from the seed, has no usable segment at all.
All inputs are finite; a program needn't handle non-finite values.
Results may differ from the reference program's by a relative error of at most 0.0043.
Values may be sent and summed in bfloat16 or wider, within the bound.
A program may use at most 128 MiB of HBM per device.

```python
import jax
import jax.numpy as jnp
from jax import lax

BLOCK = 128
SEG = 512
NB = 8
NH = 5
CHANNELS = 1024
BINS = 64


def draw_spectra(key, part):
    key = jax.random.fold_in(key, 11)
    keys = jax.random.split(key, 5)
    source = jax.random.normal(keys[0], (BINS, 2, SEG, 1), jnp.float32)
    gains = jax.random.uniform(keys[1], (1, 1, 1, CHANNELS), jnp.float32, 0.3, 1.2)
    signs = jnp.where(jax.random.normal(keys[2], (1, 1, 1, CHANNELS)) > 0, 1.0, -1.0)
    scales = jnp.exp(jax.random.uniform(keys[3], (1, 1, 1, CHANNELS), jnp.float32, 0.0, 2.3))
    noise = jax.random.normal(keys[4], (BINS, 2, SEG, CHANNELS), jnp.float32)
    return ((0.8 * source * gains * signs + noise) * scales).astype(jnp.bfloat16)


def draw_valid(key, part):
    key = jax.random.fold_in(key, 23)
    keys = jax.random.split(key, 2)
    usable = (jax.random.randint(keys[0], (NB, SEG), 0, 4) < 3).astype(jnp.int32)
    dead_block = jax.random.randint(keys[1], (), 0, NB)
    block_ids = jnp.arange(NB, dtype=jnp.int32)[:, None]
    return jnp.where(block_ids == dead_block, 0, usable).astype(jnp.int32)


def setup_inputs(seed: int = 0) -> dict:
    arg_keys = jax.random.split(jax.random.key(seed), 3)
    return {
        "spectra": draw_spectra(jax.random.fold_in(arg_keys[2], 71), 0),
        "valid": draw_valid(jax.random.fold_in(arg_keys[2], 71), 0),
    }


def reference(spectra, valid):
    spectra32 = spectra.astype(jnp.float32)
    amplitude = lax.optimization_barrier(jnp.sum(jnp.sqrt(spectra32[:, 0] ** 2 + spectra32[:, 1] ** 2), axis=0))
    keep = jnp.repeat(valid.astype(jnp.float32).T, BLOCK, axis=1)
    white = (spectra32 / (amplitude / BINS + 1e-06) * keep).astype(jnp.bfloat16)
    maskf = valid.astype(jnp.float32)

    def one_row(index):
        left = lax.dynamic_slice_in_dim(white, index * BLOCK, BLOCK, 3).astype(jnp.float32)
        left_mask = lax.dynamic_slice_in_dim(maskf, index, 1, 0)[0]
        pieces = []
        for lag in range(NH):
            other = ((index + lag) % NB).astype(jnp.int32)
            right = lax.dynamic_slice_in_dim(white, other * BLOCK, BLOCK, 3).astype(jnp.float32)
            right_mask = lax.dynamic_slice_in_dim(maskf, other, 1, 0)[0]
            total = jnp.maximum(jnp.sum(left_mask * right_mask), 1.0)
            real_part = jnp.einsum('fsa,fsb->fab', left[:, 0], right[:, 0]) + jnp.einsum('fsa,fsb->fab', left[:, 1], right[:, 1])
            imag_part = jnp.einsum('fsa,fsb->fab', left[:, 1], right[:, 0]) - jnp.einsum('fsa,fsb->fab', left[:, 0], right[:, 1])
            pieces.append((jnp.stack([real_part, imag_part], axis=1) / total).astype(jnp.bfloat16))
        return jnp.stack(pieces)
    return lax.map(one_row, jnp.arange(NB, dtype=jnp.int32))
```

```python
import functools

import jax
import jax.numpy as jnp
from jax import lax
from jax.experimental import pallas as pl
from jax.experimental.pallas import tpu as pltpu
from jax.sharding import PartitionSpec as P


def shifted(block, axis, distance):
    devices = range(lax.axis_size(axis))
    route = [((i - distance) % len(devices), i) for i in devices]
    return lax.ppermute(block, axis, route)


def cross_block(left, right, left_mask, right_mask):
    total = jnp.maximum(jnp.sum(left_mask * right_mask), 1.0)
    real_part = jnp.einsum(
        "fsa,fsb->fab", left[:, 0], right[:, 0], preferred_element_type=jnp.float32
    )
    real_part = real_part + jnp.einsum(
        "fsa,fsb->fab", left[:, 1], right[:, 1], preferred_element_type=jnp.float32
    )
    imag_part = jnp.einsum(
        "fsa,fsb->fab", left[:, 1], right[:, 0], preferred_element_type=jnp.float32
    )
    imag_part = imag_part - jnp.einsum(
        "fsa,fsb->fab", left[:, 0], right[:, 1], preferred_element_type=jnp.float32
    )
    return (jnp.stack([real_part, imag_part], axis=1) / total).astype(jnp.bfloat16)


def shards(spectra, valid):
    bin_devices = lax.axis_size("bin")
    chan_devices = lax.axis_size("chan")
    bins_here = spectra.shape[0]
    blocks_here = valid.shape[0]
    width = spectra.shape[3] // blocks_here
    block_count = blocks_here * chan_devices
    offsets = block_count // 2 + 1
    spectra32 = spectra.astype(jnp.float32)
    partial_value = jnp.sum(jnp.sqrt(spectra32[:, 0] ** 2 + spectra32[:, 1] ** 2), axis=0)
    amplitude = lax.psum(partial_value, "bin")
    keep = jnp.repeat(valid.astype(jnp.float32).T, width, axis=1)
    white = (spectra32 / (amplitude / (bins_here * bin_devices) + 1e-06) * keep).astype(
        jnp.bfloat16
    )
    own_mask = valid.astype(jnp.float32)
    results = [[None] * offsets for row_block in range(blocks_here)]

    def fill(blocks, masks, offset):
        masks_float = masks.astype(jnp.float32)
        for row_block in range(blocks_here):
            for col_block in range(blocks_here):
                lag = offset * blocks_here + col_block - row_block
                if 0 <= lag < offsets:
                    left = white[..., row_block * width : (row_block + 1) * width]
                    right = blocks[..., col_block * width : (col_block + 1) * width]
                    results[row_block][lag] = cross_block(
                        left, right, own_mask[row_block], masks_float[col_block]
                    )

    fill(white, valid, 0)
    farthest = (blocks_here - 1 + block_count // 2) // blocks_here
    moving = (white, valid)
    for offset in range(1, farthest + 1):
        moving = shifted((moving[0], moving[1]), "chan", -1)
        fill(moving[0], moving[1], offset)
    return jnp.stack([jnp.stack(row_list) for row_list in results])


def full_rows(row_block):
    return (slice(0, 3), slice(2, 5)) if row_block == 0 else (slice(3, 7), slice(1, 5))


def part_rows(row_block):
    return (slice(2, 3), slice(4, 5)) if row_block == 0 else (slice(5, 7), slice(3, 5))


def near_rows(row_block):
    return (slice(0, 2), slice(2, 4)) if row_block == 0 else (slice(2, 4), slice(1, 3))


def hub_kernel(
    total_bins, x_ref, keep_ref, vrow_ref, out_ref, part, pieces, scale, masks, outer_raw, cross_raw,
    white, stage, near_stage, raw_send, raw_recv, relay_send, cross_recv, part_send, part_recv,
    scale_send, scale_recv, col_send, col_recv, mask_send, mask_recv,
    stage_send, near_send, result_recv, near_recv, local_sem,
):
    z = lax.axis_index("chan")
    b = lax.axis_index("bin")
    peers = lax.axis_size("bin")
    bins, _, seg, chans = x_ref.shape
    width = chans // 2
    half = bins // 2
    rows = seg // peers
    is_hub = (z == 1) | (z == 2)
    is_outer = jnp.logical_not(is_hub)
    outer_hub = jnp.where(z == 0, 1, 2)
    other_hub = 3 - z
    outer = jnp.where(z == 1, 0, 3)
    other_outer = 3 - outer
    cross_base = jnp.where(z == 1, half, 0)
    relay_base = half - cross_base
    first_base = jnp.where(z == 0, 0, half)

    def peer(step):
        return (z, lax.rem(b + step, peers))

    def remote(src, dst, send, recv, device):
        return pltpu.make_async_remote_copy(
            src_ref=src, dst_ref=dst, send_sem=send, recv_sem=recv,
            device_id=device, device_id_type=pl.DeviceIdType.MESH,
        )

    barrier = pltpu.get_barrier_semaphore()
    for step in range(1, peers):
        pl.semaphore_signal(barrier, inc=1, device_id=peer(step), device_id_type=pl.DeviceIdType.MESH)
    for step in range(1, 4):
        pl.semaphore_signal(
            barrier, inc=1, device_id=(lax.rem(z + step, 4), b), device_id_type=pl.DeviceIdType.MESH
        )
    pl.semaphore_wait(barrier, peers - 1 + 3)

    def outer_send(f):
        return remote(x_ref.at[f], outer_raw.at[f], raw_send.at[f], raw_recv.at[f], (outer_hub, b))

    def own_cross(n):
        f = relay_base + n
        return remote(
            x_ref.at[f], cross_raw.at[0, n], raw_send.at[n], cross_recv.at[0, n], (other_hub, b)
        )

    def relay(n):
        return remote(
            outer_raw.at[relay_base + n], cross_raw.at[1, n], relay_send.at[n], cross_recv.at[1, n],
            (other_hub, b),
        )

    @pl.when(is_outer)
    def _():
        for n in range(half):
            outer_send(first_base + n).start()

    @pl.when(is_hub)
    def _():
        for n in range(half):
            own_cross(n).start()

    def mask_copy(hub):
        return remote(vrow_ref, masks.at[z], mask_send.at[hub - 1], mask_recv.at[z], (hub, b))

    masks[z] = vrow_ref[...]
    for hub in (1, 2):
        @pl.when(z != hub)
        def _():
            mask_copy(hub).start()

    def add_bins(i, carry):
        at = pl.ds(pl.multiple_of(i * 16, 16), 16)
        total = jnp.zeros((16, chans), jnp.float32)
        for f in range(bins):
            re = x_ref[f, 0, at, :].astype(jnp.float32)
            im = x_ref[f, 1, at, :].astype(jnp.float32)
            total = total + jnp.sqrt(re * re + im * im)
        part[at, :] = total
        return carry

    lax.fori_loop(0, seg // 16, add_bins, 0)

    def piece_rows(index):
        return pl.ds(pl.multiple_of(index * rows, rows), rows)

    def part_copy(step):
        target = peer(step)
        return remote(
            part.at[piece_rows(target[1])], pieces.at[step - 1],
            part_send.at[step - 1], part_recv.at[step - 1], target,
        )

    for step in range(1, peers):
        part_copy(step).start()

    @pl.when(is_outer)
    def _():
        for n in range(half):
            outer_send(half - first_base + n).start()

    for step in range(1, peers):
        part_copy(step).wait_recv()
    mine = piece_rows(b)
    total = part[mine, :]
    for step in range(1, peers):
        total = total + pieces[step - 1]
    scale[z, mine, :] = keep_ref[mine, :] / (total / total_bins + 1e-06)

    def scale_copy(layer, step):
        return remote(
            scale.at[layer, mine], scale.at[layer, mine],
            scale_send.at[layer, step - 1], scale_recv.at[layer, step - 1], peer(step),
        )

    def scale_arrival(layer, step):
        source = piece_rows(lax.rem(b + peers - step, peers))
        return remote(
            scale.at[layer, source], scale.at[layer, source],
            scale_send.at[layer, step - 1], scale_recv.at[layer, step - 1], peer(step),
        )

    def col_copy(hub):
        return remote(
            scale.at[z, mine], scale.at[z, mine], col_send.at[hub - 1], col_recv.at[z], (hub, b)
        )

    def col_arrival(layer):
        return remote(
            scale.at[layer, mine], scale.at[layer, mine], col_send.at[0], col_recv.at[layer],
            (lax.rem(z + 1, 4), b),
        )

    def mask_arrival(layer):
        return remote(
            vrow_ref, masks.at[layer], mask_send.at[0], mask_recv.at[layer], (lax.rem(z + 1, 4), b)
        )

    for hub in (1, 2):
        @pl.when(z != hub)
        def _():
            col_copy(hub).start()
    for step in range(1, peers):
        scale_copy(z, step).start()
    for step in range(1, peers):
        scale_arrival(z, step).wait_recv()

    def whiten(src, slot, layer):
        def chunk(i, carry):
            at = pl.ds(pl.multiple_of(i * 64, 64), 64)
            factor = scale[layer, at, :]
            for p in range(2):
                white[slot, p, at, :] = (src[p, at, :].astype(jnp.float32) * factor).astype(jnp.bfloat16)
            return carry

        lax.fori_loop(0, seg // 64, chunk, 0)

    def dot(a, c):
        return lax.dot_general(a, c, (((0,), (0,)), ((), ())), preferred_element_type=jnp.float32)

    def cross(left, right, store, wanted):
        lr, li = white[left, 0], white[left, 1]
        rr, ri = white[right, 0], white[right, 1]
        real = dot(lr, rr) + dot(li, ri)
        imag = dot(li, rr) - dot(lr, ri)
        for row, col in wanted:
            weight = masks[left, row : row + 1, :] * masks[right, col : col + 1, :]
            inverse = 1.0 / jnp.maximum(jnp.sum(weight, axis=1, keepdims=True), 1.0)
            here = (slice(row * width, (row + 1) * width), slice(col * width, (col + 1) * width))
            store(row, col, 0, (real[here] * inverse).astype(jnp.bfloat16))
            store(row, col, 1, (imag[here] * inverse).astype(jnp.bfloat16))

    def own_pairs(f):
        def store(row, col, p, value):
            out_ref[row, col - row, f, p] = value

        whiten(x_ref.at[f], z, z)
        cross(z, z, store, ((0, 0), (0, 1), (1, 1)))

    everything = ((0, 0), (0, 1), (1, 0), (1, 1))

    @pl.when(is_outer)
    def _():
        def body(f, carry):
            own_pairs(f)
            return carry

        lax.fori_loop(0, bins, body, 0)

    def near_copy(n, row):
        src, dst = near_rows(row)
        return remote(
            near_stage.at[n, src], out_ref.at[row, dst, n], near_send.at[n, row], near_recv.at[n, row],
            (0, b),
        )

    def near_local(n, row):
        src, dst = near_rows(row)
        return pltpu.make_async_copy(
            near_stage.at[n, src], out_ref.at[row, dst, relay_base + n], near_send.at[n, row]
        )

    def full_copy(n, target, row, f):
        src, dst = full_rows(row)
        return remote(
            stage.at[n, target, src], out_ref.at[row, dst, f], stage_send.at[n, target, row],
            result_recv.at[f, row], (target, b),
        )

    def part_result(n, target, row, f):
        src, dst = part_rows(row)
        return remote(
            stage.at[n, target, src], out_ref.at[row, dst, f], stage_send.at[n, target, row],
            result_recv.at[f, row], (target, b),
        )

    def local_copy(n, row):
        src, dst = full_rows(row)
        return pltpu.make_async_copy(
            stage.at[n, z, src], out_ref.at[row, dst, cross_base + n], local_sem.at[n, row]
        )

    lower = 2 * (z - 1)

    @pl.when(is_hub)
    def _():
        for distance in range(1, 4):
            layer = lax.rem(z + distance, 4)
            col_arrival(layer).wait_recv()
            for step in range(1, peers):
                scale_copy(layer, step).start()

        for distance in range(1, 4):
            layer = lax.rem(z + distance, 4)
            mask_arrival(layer).wait_recv()
            for step in range(1, peers):
                scale_arrival(layer, step).wait_recv()

        def near(n, carry):
            f = relay_base + n
            remote(x_ref.at[f], outer_raw.at[f], raw_send.at[f], raw_recv.at[f], (outer, b)).wait_recv()
            relay(n).start()
            own_pairs(f)
            whiten(outer_raw.at[f], outer, outer)

            def store(row, col, p, value):
                near_stage[n, 2 * row + col, p] = value

            cross(lower, lower + 1, store, everything)

            @pl.when(z == 1)
            def _():
                for row in range(2):
                    near_copy(n, row).start()

            @pl.when(z == 2)
            def _():
                for row in range(2):
                    near_local(n, row).start()

            return carry

        lax.fori_loop(0, half, near, 0)

        def far(n, carry):
            f = cross_base + n
            own_pairs(f)
            remote(x_ref.at[f], outer_raw.at[f], raw_send.at[f], raw_recv.at[f], (outer, b)).wait_recv()
            whiten(outer_raw.at[f], outer, outer)
            own_cross(n).wait_recv()
            whiten(cross_raw.at[0, n], other_hub, other_hub)
            relay(n).wait_recv()
            whiten(cross_raw.at[1, n], other_outer, other_outer)

            def one_row(d, inner):
                def store(row, col, p, value):
                    stage[n, d, 3 * row + col, p] = value

                def store_far(row, col, p, value):
                    stage[n, d, 2 + 3 * row + col, p] = value

                cross(d, lax.rem(d + 1, 4), store, everything)
                cross(d, lax.rem(d + 2, 4), store_far, ((0, 0), (1, 0), (1, 1)))
                return inner

            lax.fori_loop(0, 4, one_row, 0)
            for row in range(2):
                part_result(n, 4 - 2 * z, row, f).start()
                full_copy(n, 3, row, f).start()
                full_copy(n, z - 1, row, f).start()
                local_copy(n, row).start()
            return carry

        lax.fori_loop(0, half, far, 0)

    @pl.when(z == 0)
    def _():
        for n in range(half):
            for row in range(2):
                near_copy(n, row).wait_recv()
                part_result(n, 0, row, n).wait_recv()
                full_copy(n, 0, row, half + n).wait_recv()

    @pl.when(z == 1)
    def _():
        for n in range(half):
            for row in range(2):
                full_copy(n, 1, row, n).wait_recv()

    @pl.when(z == 2)
    def _():
        for n in range(half):
            for row in range(2):
                part_result(n, 2, row, half + n).wait_recv()

    @pl.when(z == 3)
    def _():
        for f in range(bins):
            for row in range(2):
                full_copy(f % half, 3, row, f).wait_recv()

    @pl.when(is_outer)
    def _():
        for f in range(bins):
            outer_send(f).wait_send()

    @pl.when(is_hub)
    def _():
        for n in range(half):
            own_cross(n).wait_send()
            relay(n).wait_send()
            for row in range(2):
                f = cross_base + n
                part_result(n, 4 - 2 * z, row, f).wait_send()
                full_copy(n, 3, row, f).wait_send()
                full_copy(n, z - 1, row, f).wait_send()
                local_copy(n, row).wait()
        for distance in range(1, 4):
            for step in range(1, peers):
                scale_copy(lax.rem(z + distance, 4), step).wait_send()

    @pl.when(z == 1)
    def _():
        for n in range(half):
            for row in range(2):
                near_copy(n, row).wait_send()

    @pl.when(z == 2)
    def _():
        for n in range(half):
            for row in range(2):
                near_local(n, row).wait()

    for hub in (1, 2):
        @pl.when(z != hub)
        def _():
            mask_copy(hub).wait_send()
            col_copy(hub).wait_send()
    for step in range(1, peers):
        part_copy(step).wait_send()
        scale_copy(z, step).wait_send()


def hub_shards(spectra, valid):
    peers = lax.axis_size("bin")
    bins, _, seg, chans = spectra.shape
    width = chans // 2
    half = bins // 2
    valid_float = valid.astype(jnp.float32)
    keep = jnp.repeat(valid_float.T, width, axis=1)
    rows = jnp.tile(valid_float, (4, 1))
    dma = pltpu.SemaphoreType.DMA
    vmem = pl.BlockSpec(memory_space=pltpu.VMEM)
    block = (2, seg, chans)
    result = (2, width, width)
    return pl.pallas_call(
        functools.partial(hub_kernel, bins * peers),
        out_shape=jax.ShapeDtypeStruct((2, 5, bins) + result, jnp.bfloat16),
        in_specs=[vmem] * 3,
        out_specs=vmem,
        scratch_shapes=[
            pltpu.VMEM((seg, chans), jnp.float32),
            pltpu.VMEM((peers - 1, seg // peers, chans), jnp.float32),
            pltpu.VMEM((4, seg, chans), jnp.float32),
            pltpu.VMEM((4, 8, seg), jnp.float32),
            pltpu.VMEM((bins,) + block, jnp.bfloat16),
            pltpu.VMEM((2, half) + block, jnp.bfloat16),
            pltpu.VMEM((4,) + block, jnp.bfloat16),
            pltpu.VMEM((half, 4, 7) + result, jnp.bfloat16),
            pltpu.VMEM((half, 4) + result, jnp.bfloat16),
            dma((bins,)), dma((bins,)), dma((half,)), dma((2, half)),
            dma((peers - 1,)), dma((peers - 1,)),
            dma((4, peers - 1)), dma((4, peers - 1)), dma((2,)), dma((4,)), dma((2,)), dma((4,)),
            dma((half, 4, 2)), dma((half, 2)), dma((bins, 2)), dma((half, 2)), dma((half, 2)),
        ],
        compiler_params=pltpu.CompilerParams(
            collective_id=0, has_side_effects=True, vmem_limit_bytes=56 * 2**20
        ),
        cost_estimate=pl.CostEstimate(
            flops=40 * bins * 2 * seg * width * width * 8, bytes_accessed=2 * spectra.size * 4,
            transcendentals=spectra.size // 2,
        ),
    )(spectra, keep, rows)


def solution(mesh):
    in_line = mesh.shape["chan"] == 4
    return jax.shard_map(
        hub_shards if in_line else shards,
        mesh=mesh,
        in_specs=(P("bin", None, None, "chan"), P("chan", None)),
        out_specs=P("chan", None, "bin", None, None, None),
        check_vma=False,
    )
```

```python
import functools

import jax
import jax.numpy as jnp
from jax import lax
from jax.experimental import pallas as pl
from jax.experimental.pallas import tpu as pltpu
from jax.sharding import PartitionSpec as P


def shifted(block, axis, distance):
    devices = range(lax.axis_size(axis))
    route = [((i - distance) % len(devices), i) for i in devices]
    return lax.ppermute(block, axis, route)


def cross_block(left, right, left_mask, right_mask):
    total = jnp.maximum(jnp.sum(left_mask * right_mask), 1.0)
    real_part = jnp.einsum(
        "fsa,fsb->fab", left[:, 0], right[:, 0], preferred_element_type=jnp.float32
    )
    real_part = real_part + jnp.einsum(
        "fsa,fsb->fab", left[:, 1], right[:, 1], preferred_element_type=jnp.float32
    )
    imag_part = jnp.einsum(
        "fsa,fsb->fab", left[:, 1], right[:, 0], preferred_element_type=jnp.float32
    )
    imag_part = imag_part - jnp.einsum(
        "fsa,fsb->fab", left[:, 0], right[:, 1], preferred_element_type=jnp.float32
    )
    return (jnp.stack([real_part, imag_part], axis=1) / total).astype(jnp.bfloat16)


def shards(spectra, valid):
    bin_devices = lax.axis_size("bin")
    chan_devices = lax.axis_size("chan")
    bins_here = spectra.shape[0]
    blocks_here = valid.shape[0]
    width = spectra.shape[3] // blocks_here
    block_count = blocks_here * chan_devices
    offsets = block_count // 2 + 1
    spectra32 = spectra.astype(jnp.float32)
    partial_value = jnp.sum(jnp.sqrt(spectra32[:, 0] ** 2 + spectra32[:, 1] ** 2), axis=0)
    amplitude = lax.psum(partial_value, "bin")
    keep = jnp.repeat(valid.astype(jnp.float32).T, width, axis=1)
    white = (spectra32 / (amplitude / (bins_here * bin_devices) + 1e-06) * keep).astype(
        jnp.bfloat16
    )
    own_mask = valid.astype(jnp.float32)
    results = [[None] * offsets for row_block in range(blocks_here)]

    def fill(blocks, masks, offset):
        masks_float = masks.astype(jnp.float32)
        for row_block in range(blocks_here):
            for col_block in range(blocks_here):
                lag = offset * blocks_here + col_block - row_block
                if 0 <= lag < offsets:
                    left = white[..., row_block * width : (row_block + 1) * width]
                    right = blocks[..., col_block * width : (col_block + 1) * width]
                    results[row_block][lag] = cross_block(
                        left, right, own_mask[row_block], masks_float[col_block]
                    )

    fill(white, valid, 0)
    farthest = (blocks_here - 1 + block_count // 2) // blocks_here
    moving = (white, valid)
    for offset in range(1, farthest + 1):
        moving = shifted((moving[0], moving[1]), "chan", -1)
        fill(moving[0], moving[1], offset)
    return jnp.stack([jnp.stack(row_list) for row_list in results])


def full_rows(row_block):
    return (slice(0, 3), slice(2, 5)) if row_block == 0 else (slice(3, 7), slice(1, 5))


def part_rows(row_block):
    return (slice(2, 3), slice(4, 5)) if row_block == 0 else (slice(5, 7), slice(3, 5))


def near_rows(row_block):
    return (slice(0, 2), slice(2, 4)) if row_block == 0 else (slice(2, 4), slice(1, 3))


def hub_kernel(
    total_bins, x_ref, keep_ref, vrow_ref, out_ref, part, pieces, scale, masks, outer_raw, cross_raw,
    white, stage, near_stage, raw_send, raw_recv, relay_send, cross_recv, part_send, part_recv,
    scale_send, scale_recv, col_send, col_recv, mask_send, mask_recv,
    stage_send, near_send, result_recv, near_recv, local_sem,
):
    z = lax.axis_index("chan")
    b = lax.axis_index("bin")
    peers = lax.axis_size("bin")
    bins, _, seg, chans = x_ref.shape
    width = chans // 2
    half = bins // 2
    rows = seg // peers
    is_hub = (z == 1) | (z == 2)
    is_outer = jnp.logical_not(is_hub)
    outer_hub = jnp.where(z == 0, 1, 2)
    other_hub = 3 - z
    outer = jnp.where(z == 1, 0, 3)
    other_outer = 3 - outer
    cross_base = jnp.where(z == 1, half, 0)
    relay_base = half - cross_base
    first_base = jnp.where(z == 0, 0, half)

    def peer(step):
        return (z, lax.rem(b + step, peers))

    def remote(src, dst, send, recv, device):
        return pltpu.make_async_remote_copy(
            src_ref=src, dst_ref=dst, send_sem=send, recv_sem=recv,
            device_id=device, device_id_type=pl.DeviceIdType.MESH,
        )

    barrier = pltpu.get_barrier_semaphore()
    for step in range(1, peers):
        pl.semaphore_signal(barrier, inc=1, device_id=peer(step), device_id_type=pl.DeviceIdType.MESH)
    for step in range(1, 4):
        pl.semaphore_signal(
            barrier, inc=1, device_id=(lax.rem(z + step, 4), b), device_id_type=pl.DeviceIdType.MESH
        )
    pl.semaphore_wait(barrier, peers - 1 + 3)

    def outer_send(f):
        return remote(x_ref.at[f], outer_raw.at[f], raw_send.at[f], raw_recv.at[f], (outer_hub, b))

    def outer_arrival(f):
        return remote(x_ref.at[f], outer_raw.at[f], raw_send.at[f], raw_recv.at[f], (outer, b))

    def own_cross(n):
        f = relay_base + n
        return remote(
            x_ref.at[f], cross_raw.at[0, n], raw_send.at[n], cross_recv.at[0, n], (other_hub, b)
        )

    def relay(n):
        return remote(
            outer_raw.at[relay_base + n], cross_raw.at[1, n], relay_send.at[n], cross_recv.at[1, n],
            (other_hub, b),
        )

    @pl.when(is_outer)
    def _():
        for n in range(half - 1):
            outer_send(first_base + n).start()

    @pl.when(is_hub)
    def _():
        for n in range(half // 2):
            own_cross(n).start()

    def mask_copy(hub):
        return remote(vrow_ref, masks.at[z], mask_send.at[hub - 1], mask_recv.at[z], (hub, b))

    masks[z] = vrow_ref[...]
    for hub in (1, 2):
        @pl.when(z != hub)
        def _():
            mask_copy(hub).start()

    def add_bins(i, carry):
        at = pl.ds(pl.multiple_of(i * 16, 16), 16)
        total = jnp.zeros((16, chans), jnp.float32)
        for f in range(bins):
            re = x_ref[f, 0, at, :].astype(jnp.float32)
            im = x_ref[f, 1, at, :].astype(jnp.float32)
            total = total + jnp.sqrt(re * re + im * im)
        part[at, :] = total
        return carry

    lax.fori_loop(0, seg // 16, add_bins, 0)

    def piece_rows(index):
        return pl.ds(pl.multiple_of(index * rows, rows), rows)

    def part_copy(step):
        target = peer(step)
        return remote(
            part.at[piece_rows(target[1])], pieces.at[step - 1],
            part_send.at[step - 1], part_recv.at[step - 1], target,
        )

    for step in range(1, peers):
        part_copy(step).start()

    @pl.when(is_hub)
    def _():
        for n in range(half // 2, half - 1):
            own_cross(n).start()

    for step in range(1, peers):
        part_copy(step).wait_recv()
    mine = piece_rows(b)
    total = part[mine, :]
    for step in range(1, peers):
        total = total + pieces[step - 1]
    scale[z, mine, :] = keep_ref[mine, :] / (total / total_bins + 1e-06)

    def scale_copy(layer, step):
        return remote(
            scale.at[layer, mine], scale.at[layer, mine],
            scale_send.at[layer, step - 1], scale_recv.at[layer, step - 1], peer(step),
        )

    def scale_arrival(layer, step):
        source = piece_rows(lax.rem(b + peers - step, peers))
        return remote(
            scale.at[layer, source], scale.at[layer, source],
            scale_send.at[layer, step - 1], scale_recv.at[layer, step - 1], peer(step),
        )

    def col_copy(hub):
        return remote(
            scale.at[z, mine], scale.at[z, mine], col_send.at[hub - 1], col_recv.at[z], (hub, b)
        )

    def col_arrival(layer):
        return remote(
            scale.at[layer, mine], scale.at[layer, mine], col_send.at[0], col_recv.at[layer],
            (lax.rem(z + 1, 4), b),
        )

    def mask_arrival(layer):
        return remote(
            vrow_ref, masks.at[layer], mask_send.at[0], mask_recv.at[layer], (lax.rem(z + 1, 4), b)
        )

    for hub in (1, 2):
        @pl.when(z != hub)
        def _():
            col_copy(hub).start()
    for step in range(1, peers):
        scale_copy(z, step).start()

    @pl.when(is_outer)
    def _():
        outer_send(first_base + half - 1).start()
        for n in range(half):
            outer_send(half - first_base + n).start()

    @pl.when(is_hub)
    def _():
        own_cross(half - 1).start()
        for n in range(half):
            outer_arrival(relay_base + n).wait_recv()
            relay(n).start()

    for step in range(1, peers):
        scale_arrival(z, step).wait_recv()

    def whiten(src, slot, layer):
        def chunk(i, carry):
            at = pl.ds(pl.multiple_of(i * 64, 64), 64)
            factor = scale[layer, at, :]
            for p in range(2):
                white[slot, p, at, :] = (src[p, at, :].astype(jnp.float32) * factor).astype(jnp.bfloat16)
            return carry

        lax.fori_loop(0, seg // 64, chunk, 0)

    def dot(a, c):
        return lax.dot_general(a, c, (((0,), (0,)), ((), ())), preferred_element_type=jnp.float32)

    def cross(left, right, store, wanted):
        lr, li = white[left, 0], white[left, 1]
        rr, ri = white[right, 0], white[right, 1]
        real = dot(lr, rr) + dot(li, ri)
        imag = dot(li, rr) - dot(lr, ri)
        for row, col in wanted:
            weight = masks[left, row : row + 1, :] * masks[right, col : col + 1, :]
            inverse = 1.0 / jnp.maximum(jnp.sum(weight, axis=1, keepdims=True), 1.0)
            here = (slice(row * width, (row + 1) * width), slice(col * width, (col + 1) * width))
            store(row, col, 0, (real[here] * inverse).astype(jnp.bfloat16))
            store(row, col, 1, (imag[here] * inverse).astype(jnp.bfloat16))

    def own_pairs(f):
        def store(row, col, p, value):
            out_ref[row, col - row, f, p] = value

        whiten(x_ref.at[f], z, z)
        cross(z, z, store, ((0, 0), (0, 1), (1, 1)))

    everything = ((0, 0), (0, 1), (1, 0), (1, 1))

    @pl.when(is_outer)
    def _():
        def body(f, carry):
            own_pairs(f)
            return carry

        lax.fori_loop(0, bins, body, 0)

    def near_copy(n, row):
        src, dst = near_rows(row)
        return remote(
            near_stage.at[n, src], out_ref.at[row, dst, n], near_send.at[n, row], near_recv.at[n, row],
            (0, b),
        )

    def near_local(n, row):
        src, dst = near_rows(row)
        return pltpu.make_async_copy(
            near_stage.at[n, src], out_ref.at[row, dst, relay_base + n], near_send.at[n, row]
        )

    def full_copy(n, target, row, f):
        src, dst = full_rows(row)
        return remote(
            stage.at[n, target, src], out_ref.at[row, dst, f], stage_send.at[n, target, row],
            result_recv.at[f, row], (target, b),
        )

    def part_result(n, target, row, f):
        src, dst = part_rows(row)
        return remote(
            stage.at[n, target, src], out_ref.at[row, dst, f], stage_send.at[n, target, row],
            result_recv.at[f, row], (target, b),
        )

    def local_copy(n, row):
        src, dst = full_rows(row)
        return pltpu.make_async_copy(
            stage.at[n, z, src], out_ref.at[row, dst, cross_base + n], local_sem.at[n, row]
        )

    lower = 2 * (z - 1)

    @pl.when(is_hub)
    def _():
        for layer in (outer, other_hub, other_outer):
            col_arrival(layer).wait_recv()
            for step in range(1, peers):
                scale_copy(layer, step).start()

        def layer_arrival(layer):
            mask_arrival(layer).wait_recv()
            for step in range(1, peers):
                scale_arrival(layer, step).wait_recv()

        layer_arrival(outer)

        def near(n, carry):
            f = relay_base + n
            own_pairs(f)
            whiten(outer_raw.at[f], outer, outer)

            def store(row, col, p, value):
                near_stage[n, 2 * row + col, p] = value

            cross(lower, lower + 1, store, everything)

            @pl.when(z == 1)
            def _():
                for row in range(2):
                    near_copy(n, row).start()

            @pl.when(z == 2)
            def _():
                for row in range(2):
                    near_local(n, row).start()

            return carry

        lax.fori_loop(0, half, near, 0)
        layer_arrival(other_hub)
        layer_arrival(other_outer)

        def far(n, carry):
            f = cross_base + n
            own_pairs(f)
            outer_arrival(f).wait_recv()
            whiten(outer_raw.at[f], outer, outer)
            own_cross(n).wait_recv()
            whiten(cross_raw.at[0, n], other_hub, other_hub)
            relay(n).wait_recv()
            whiten(cross_raw.at[1, n], other_outer, other_outer)

            def one_row(d, inner):
                def store(row, col, p, value):
                    stage[n, d, 3 * row + col, p] = value

                def store_far(row, col, p, value):
                    stage[n, d, 2 + 3 * row + col, p] = value

                cross(d, lax.rem(d + 1, 4), store, everything)
                cross(d, lax.rem(d + 2, 4), store_far, ((0, 0), (1, 0), (1, 1)))
                return inner

            lax.fori_loop(0, 4, one_row, 0)
            for row in range(2):
                part_result(n, 4 - 2 * z, row, f).start()
                full_copy(n, 3, row, f).start()
                full_copy(n, z - 1, row, f).start()
                local_copy(n, row).start()
            return carry

        lax.fori_loop(0, half, far, 0)

    @pl.when(z == 0)
    def _():
        for n in range(half):
            for row in range(2):
                near_copy(n, row).wait_recv()
                part_result(n, 0, row, n).wait_recv()
                full_copy(n, 0, row, half + n).wait_recv()

    @pl.when(z == 1)
    def _():
        for n in range(half):
            for row in range(2):
                full_copy(n, 1, row, n).wait_recv()

    @pl.when(z == 2)
    def _():
        for n in range(half):
            for row in range(2):
                part_result(n, 2, row, half + n).wait_recv()

    @pl.when(z == 3)
    def _():
        for f in range(bins):
            for row in range(2):
                full_copy(f % half, 3, row, f).wait_recv()

    @pl.when(is_outer)
    def _():
        for f in range(bins):
            outer_send(f).wait_send()

    @pl.when(is_hub)
    def _():
        for n in range(half):
            own_cross(n).wait_send()
            relay(n).wait_send()
            for row in range(2):
                f = cross_base + n
                part_result(n, 4 - 2 * z, row, f).wait_send()
                full_copy(n, 3, row, f).wait_send()
                full_copy(n, z - 1, row, f).wait_send()
                local_copy(n, row).wait()
        for distance in range(1, 4):
            for step in range(1, peers):
                scale_copy(lax.rem(z + distance, 4), step).wait_send()

    @pl.when(z == 1)
    def _():
        for n in range(half):
            for row in range(2):
                near_copy(n, row).wait_send()

    @pl.when(z == 2)
    def _():
        for n in range(half):
            for row in range(2):
                near_local(n, row).wait()

    for hub in (1, 2):
        @pl.when(z != hub)
        def _():
            mask_copy(hub).wait_send()
            col_copy(hub).wait_send()
    for step in range(1, peers):
        part_copy(step).wait_send()
        scale_copy(z, step).wait_send()


def hub_shards(spectra, valid):
    peers = lax.axis_size("bin")
    bins, _, seg, chans = spectra.shape
    width = chans // 2
    half = bins // 2
    valid_float = valid.astype(jnp.float32)
    keep = jnp.repeat(valid_float.T, width, axis=1)
    rows = jnp.tile(valid_float, (4, 1))
    dma = pltpu.SemaphoreType.DMA
    vmem = pl.BlockSpec(memory_space=pltpu.VMEM)
    block = (2, seg, chans)
    result = (2, width, width)
    return pl.pallas_call(
        functools.partial(hub_kernel, bins * peers),
        out_shape=jax.ShapeDtypeStruct((2, 5, bins) + result, jnp.bfloat16),
        in_specs=[vmem] * 3,
        out_specs=vmem,
        scratch_shapes=[
            pltpu.VMEM((seg, chans), jnp.float32),
            pltpu.VMEM((peers - 1, seg // peers, chans), jnp.float32),
            pltpu.VMEM((4, seg, chans), jnp.float32),
            pltpu.VMEM((4, 8, seg), jnp.float32),
            pltpu.VMEM((bins,) + block, jnp.bfloat16),
            pltpu.VMEM((2, half) + block, jnp.bfloat16),
            pltpu.VMEM((4,) + block, jnp.bfloat16),
            pltpu.VMEM((half, 4, 7) + result, jnp.bfloat16),
            pltpu.VMEM((half, 4) + result, jnp.bfloat16),
            dma((bins,)), dma((bins,)), dma((half,)), dma((2, half)),
            dma((peers - 1,)), dma((peers - 1,)),
            dma((4, peers - 1)), dma((4, peers - 1)), dma((2,)), dma((4,)), dma((2,)), dma((4,)),
            dma((half, 4, 2)), dma((half, 2)), dma((bins, 2)), dma((half, 2)), dma((half, 2)),
        ],
        compiler_params=pltpu.CompilerParams(
            collective_id=0, has_side_effects=True, vmem_limit_bytes=56 * 2**20
        ),
        cost_estimate=pl.CostEstimate(
            flops=40 * bins * 2 * seg * width * width * 8, bytes_accessed=2 * spectra.size * 4,
            transcendentals=spectra.size // 2,
        ),
    )(spectra, keep, rows)


def solution(mesh):
    in_line = mesh.shape["chan"] == 4
    return jax.shard_map(
        hub_shards if in_line else shards,
        mesh=mesh,
        in_specs=(P("bin", None, None, "chan"), P("chan", None)),
        out_specs=P("chan", None, "bin", None, None, None),
        check_vma=False,
    )
```

```python
import functools

import jax
import jax.numpy as jnp
from jax import lax
from jax.experimental import pallas as pl
from jax.experimental.pallas import tpu as pltpu
from jax.sharding import PartitionSpec as P


def shifted(block, axis, distance):
    devices = range(lax.axis_size(axis))
    route = [((i - distance) % len(devices), i) for i in devices]
    return lax.ppermute(block, axis, route)


def cross_block(left, right, left_mask, right_mask):
    total = jnp.maximum(jnp.sum(left_mask * right_mask), 1.0)
    real_part = jnp.einsum(
        "fsa,fsb->fab", left[:, 0], right[:, 0], preferred_element_type=jnp.float32
    )
    real_part = real_part + jnp.einsum(
        "fsa,fsb->fab", left[:, 1], right[:, 1], preferred_element_type=jnp.float32
    )
    imag_part = jnp.einsum(
        "fsa,fsb->fab", left[:, 1], right[:, 0], preferred_element_type=jnp.float32
    )
    imag_part = imag_part - jnp.einsum(
        "fsa,fsb->fab", left[:, 0], right[:, 1], preferred_element_type=jnp.float32
    )
    return (jnp.stack([real_part, imag_part], axis=1) / total).astype(jnp.bfloat16)


def shards(spectra, valid):
    bin_devices = lax.axis_size("bin")
    chan_devices = lax.axis_size("chan")
    bins_here = spectra.shape[0]
    blocks_here = valid.shape[0]
    width = spectra.shape[3] // blocks_here
    block_count = blocks_here * chan_devices
    offsets = block_count // 2 + 1
    spectra32 = spectra.astype(jnp.float32)
    partial_value = jnp.sum(jnp.sqrt(spectra32[:, 0] ** 2 + spectra32[:, 1] ** 2), axis=0)
    amplitude = lax.psum(partial_value, "bin")
    keep = jnp.repeat(valid.astype(jnp.float32).T, width, axis=1)
    white = (spectra32 / (amplitude / (bins_here * bin_devices) + 1e-06) * keep).astype(
        jnp.bfloat16
    )
    own_mask = valid.astype(jnp.float32)
    results = [[None] * offsets for row_block in range(blocks_here)]

    def fill(blocks, masks, offset):
        masks_float = masks.astype(jnp.float32)
        for row_block in range(blocks_here):
            for col_block in range(blocks_here):
                lag = offset * blocks_here + col_block - row_block
                if 0 <= lag < offsets:
                    left = white[..., row_block * width : (row_block + 1) * width]
                    right = blocks[..., col_block * width : (col_block + 1) * width]
                    results[row_block][lag] = cross_block(
                        left, right, own_mask[row_block], masks_float[col_block]
                    )

    fill(white, valid, 0)
    farthest = (blocks_here - 1 + block_count // 2) // blocks_here
    moving = (white, valid)
    for offset in range(1, farthest + 1):
        moving = shifted((moving[0], moving[1]), "chan", -1)
        fill(moving[0], moving[1], offset)
    return jnp.stack([jnp.stack(row_list) for row_list in results])


def full_rows(row_block):
    return (slice(0, 3), slice(2, 5)) if row_block == 0 else (slice(3, 7), slice(1, 5))


def part_rows(row_block):
    return (slice(2, 3), slice(4, 5)) if row_block == 0 else (slice(5, 7), slice(3, 5))


def near_rows(row_block):
    return (slice(0, 2), slice(2, 4)) if row_block == 0 else (slice(2, 4), slice(1, 3))


def hub_kernel(
    total_bins, x_ref, keep_ref, vrow_ref, out_ref, part, pieces, scale, masks, outer_raw, cross_raw,
    white, stage, near_stage, raw_send, raw_recv, relay_send, cross_recv, part_send, part_recv,
    scale_send, scale_recv, col_send, col_recv, mask_send, mask_recv,
    stage_send, near_send, result_recv, near_recv, local_sem,
):
    z = lax.axis_index("chan")
    b = lax.axis_index("bin")
    peers = lax.axis_size("bin")
    bins, _, seg, chans = x_ref.shape
    width = chans // 2
    half = bins // 2
    rows = seg // peers
    is_hub = (z == 1) | (z == 2)
    is_outer = jnp.logical_not(is_hub)
    outer_hub = jnp.where(z == 0, 1, 2)
    other_hub = 3 - z
    outer = jnp.where(z == 1, 0, 3)
    other_outer = 3 - outer
    cross_base = jnp.where(z == 1, half, 0)
    relay_base = half - cross_base
    first_base = jnp.where(z == 0, 0, half)

    def peer(step):
        return (z, lax.rem(b + step, peers))

    def remote(src, dst, send, recv, device):
        return pltpu.make_async_remote_copy(
            src_ref=src, dst_ref=dst, send_sem=send, recv_sem=recv,
            device_id=device, device_id_type=pl.DeviceIdType.MESH,
        )

    barrier = pltpu.get_barrier_semaphore()
    for step in range(1, peers):
        pl.semaphore_signal(barrier, inc=1, device_id=peer(step), device_id_type=pl.DeviceIdType.MESH)
    for step in range(1, 4):
        pl.semaphore_signal(
            barrier, inc=1, device_id=(lax.rem(z + step, 4), b), device_id_type=pl.DeviceIdType.MESH
        )
    pl.semaphore_wait(barrier, peers - 1 + 3)

    def outer_send(f):
        return remote(x_ref.at[f], outer_raw.at[f], raw_send.at[f], raw_recv.at[f], (outer_hub, b))

    def outer_arrival(f):
        return remote(x_ref.at[f], outer_raw.at[f], raw_send.at[f], raw_recv.at[f], (outer, b))

    def own_cross(n):
        f = relay_base + n
        return remote(
            x_ref.at[f], cross_raw.at[0, n], raw_send.at[n], cross_recv.at[0, n], (other_hub, b)
        )

    def relay(n):
        return remote(
            outer_raw.at[relay_base + n], cross_raw.at[1, n], relay_send.at[n], cross_recv.at[1, n],
            (other_hub, b),
        )

    @pl.when(is_outer)
    def _():
        for n in range(half - 1):
            outer_send(first_base + n).start()

    @pl.when(is_hub)
    def _():
        for n in range(half // 2):
            own_cross(n).start()

    def mask_copy(hub):
        return remote(vrow_ref, masks.at[z], mask_send.at[hub - 1], mask_recv.at[z], (hub, b))

    masks[z] = vrow_ref[...]
    for hub in (1, 2):
        @pl.when(z != hub)
        def _():
            mask_copy(hub).start()

    def add_bins(i, carry):
        at = pl.ds(pl.multiple_of(i * 16, 16), 16)
        total = jnp.zeros((16, chans), jnp.float32)
        for f in range(bins):
            re = x_ref[f, 0, at, :].astype(jnp.float32)
            im = x_ref[f, 1, at, :].astype(jnp.float32)
            total = total + jnp.sqrt(re * re + im * im)
        part[at, :] = total
        return carry

    lax.fori_loop(0, seg // 16, add_bins, 0)

    def piece_rows(index):
        return pl.ds(pl.multiple_of(index * rows, rows), rows)

    def part_copy(step):
        target = peer(step)
        return remote(
            part.at[piece_rows(target[1])], pieces.at[step - 1],
            part_send.at[step - 1], part_recv.at[step - 1], target,
        )

    for step in range(1, peers):
        part_copy(step).start()

    @pl.when(is_hub)
    def _():
        for n in range(half // 2, half - 1):
            own_cross(n).start()

    for step in range(1, peers):
        part_copy(step).wait_recv()
    mine = piece_rows(b)
    total = part[mine, :]
    for step in range(1, peers):
        total = total + pieces[step - 1]
    scale[z, mine, :] = keep_ref[mine, :] / (total / total_bins + 1e-06)

    def scale_copy(layer, step):
        return remote(
            scale.at[layer, mine], scale.at[layer, mine],
            scale_send.at[layer, step - 1], scale_recv.at[layer, step - 1], peer(step),
        )

    def scale_arrival(layer, step):
        source = piece_rows(lax.rem(b + peers - step, peers))
        return remote(
            scale.at[layer, source], scale.at[layer, source],
            scale_send.at[layer, step - 1], scale_recv.at[layer, step - 1], peer(step),
        )

    def col_copy(hub):
        return remote(
            scale.at[z, mine], scale.at[z, mine], col_send.at[hub - 1], col_recv.at[z], (hub, b)
        )

    def col_arrival(layer):
        return remote(
            scale.at[layer, mine], scale.at[layer, mine], col_send.at[0], col_recv.at[layer],
            (lax.rem(z + 1, 4), b),
        )

    def mask_arrival(layer):
        return remote(
            vrow_ref, masks.at[layer], mask_send.at[0], mask_recv.at[layer], (lax.rem(z + 1, 4), b)
        )

    for hub in (1, 2):
        @pl.when(z != hub)
        def _():
            col_copy(hub).start()
    for step in range(1, peers):
        scale_copy(z, step).start()

    @pl.when(is_outer)
    def _():
        outer_send(first_base + half - 1).start()
        for n in range(half):
            outer_send(half - first_base + n).start()

    @pl.when(is_hub)
    def _():
        own_cross(half - 1).start()
        for n in range(half):
            outer_arrival(relay_base + n).wait_recv()
            relay(n).start()

    for step in range(1, peers):
        scale_arrival(z, step).wait_recv()

    def whiten(src, slot, layer):
        def chunk(i, carry):
            at = pl.ds(pl.multiple_of(i * 64, 64), 64)
            factor = scale[layer, at, :]
            for p in range(2):
                white[slot, p, at, :] = (src[p, at, :].astype(jnp.float32) * factor).astype(jnp.bfloat16)
            return carry

        lax.fori_loop(0, seg // 64, chunk, 0)

    def dot(a, c):
        return lax.dot_general(a, c, (((0,), (0,)), ((), ())), preferred_element_type=jnp.float32)

    def cross(left, right, store, wanted):
        lr, li = white[left, 0], white[left, 1]
        rr, ri = white[right, 0], white[right, 1]
        real = dot(lr, rr) + dot(li, ri)
        imag = dot(li, rr) - dot(lr, ri)
        for row, col in wanted:
            weight = masks[left, row : row + 1, :] * masks[right, col : col + 1, :]
            inverse = 1.0 / jnp.maximum(jnp.sum(weight, axis=1, keepdims=True), 1.0)
            here = (slice(row * width, (row + 1) * width), slice(col * width, (col + 1) * width))
            store(row, col, 0, (real[here] * inverse).astype(jnp.bfloat16))
            store(row, col, 1, (imag[here] * inverse).astype(jnp.bfloat16))

    def own_pairs(f):
        def store(row, col, p, value):
            out_ref[row, col - row, f, p] = value

        whiten(x_ref.at[f], z, z)
        cross(z, z, store, ((0, 0), (0, 1), (1, 1)))

    everything = ((0, 0), (0, 1), (1, 0), (1, 1))

    @pl.when(is_outer)
    def _():
        def body(f, carry):
            own_pairs(f)
            return carry

        lax.fori_loop(0, bins, body, 0)

    def near_copy(n, row):
        src, dst = near_rows(row)
        return remote(
            near_stage.at[n, src], out_ref.at[row, dst, n], near_send.at[n, row], near_recv.at[n, row],
            (0, b),
        )

    def near_local(n, row):
        src, dst = near_rows(row)
        return pltpu.make_async_copy(
            near_stage.at[n, src], out_ref.at[row, dst, relay_base + n], near_send.at[n, row]
        )

    def full_copy(n, target, row, f):
        src, dst = full_rows(row)
        return remote(
            stage.at[n, target, src], out_ref.at[row, dst, f], stage_send.at[n, target, row],
            result_recv.at[f, row], (target, b),
        )

    def part_result(n, target, row, f):
        src, dst = part_rows(row)
        return remote(
            stage.at[n, target, src], out_ref.at[row, dst, f], stage_send.at[n, target, row],
            result_recv.at[f, row], (target, b),
        )

    def local_copy(n, row):
        src, dst = full_rows(row)
        return pltpu.make_async_copy(
            stage.at[n, z, src], out_ref.at[row, dst, cross_base + n], local_sem.at[n, row]
        )

    lower = 2 * (z - 1)

    @pl.when(is_hub)
    def _():
        for layer in (outer, other_hub, other_outer):
            col_arrival(layer).wait_recv()
            for step in range(1, peers):
                scale_copy(layer, step).start()

        def layer_arrival(layer):
            mask_arrival(layer).wait_recv()
            for step in range(1, peers):
                scale_arrival(layer, step).wait_recv()

        layer_arrival(outer)

        def near(n, carry):
            f = relay_base + n
            own_pairs(f)
            whiten(outer_raw.at[f], outer, outer)

            def store(row, col, p, value):
                near_stage[n, 2 * row + col, p] = value

            cross(lower, lower + 1, store, everything)

            @pl.when(z == 1)
            def _():
                for row in range(2):
                    near_copy(n, row).start()

            @pl.when(z == 2)
            def _():
                for row in range(2):
                    near_local(n, row).start()

            return carry

        lax.fori_loop(0, half, near, 0)
        layer_arrival(other_hub)
        layer_arrival(other_outer)

        def far(n, carry):
            f = cross_base + n
            own_pairs(f)
            outer_arrival(f).wait_recv()
            whiten(outer_raw.at[f], outer, outer)
            own_cross(n).wait_recv()
            whiten(cross_raw.at[0, n], other_hub, other_hub)
            relay(n).wait_recv()
            whiten(cross_raw.at[1, n], other_outer, other_outer)

            def near_row(d):
                def store(row, col, p, value):
                    stage[n, d, 3 * row + col, p] = value

                cross(d, lax.rem(d + 1, 4), store, everything)

            def far_row(d):
                def store(row, col, p, value):
                    stage[n, d, 2 + 3 * row + col, p] = value

                cross(d, lax.rem(d + 2, 4), store, ((0, 0), (1, 0), (1, 1)))

            near_row(5 - 2 * z)
            far_row(5 - 2 * z)
            for row in range(2):
                full_copy(n, 5 - 2 * z, row, f).start()
            far_row(4 - 2 * z)
            for row in range(2):
                part_result(n, 4 - 2 * z, row, f).start()

            def one_row(j, inner):
                d = jnp.where(j == 0, 3 * z - 3, z)
                near_row(d)
                far_row(d)
                return inner

            lax.fori_loop(0, 2, one_row, 0)
            for row in range(2):
                full_copy(n, 3 * z - 3, row, f).start()
                local_copy(n, row).start()
            return carry

        lax.fori_loop(0, half, far, 0)

    @pl.when(z == 0)
    def _():
        for n in range(half):
            for row in range(2):
                near_copy(n, row).wait_recv()
                part_result(n, 0, row, n).wait_recv()
                full_copy(n, 0, row, half + n).wait_recv()

    @pl.when(z == 1)
    def _():
        for n in range(half):
            for row in range(2):
                full_copy(n, 1, row, n).wait_recv()

    @pl.when(z == 2)
    def _():
        for n in range(half):
            for row in range(2):
                part_result(n, 2, row, half + n).wait_recv()

    @pl.when(z == 3)
    def _():
        for f in range(bins):
            for row in range(2):
                full_copy(f % half, 3, row, f).wait_recv()

    @pl.when(is_outer)
    def _():
        for f in range(bins):
            outer_send(f).wait_send()

    @pl.when(is_hub)
    def _():
        for n in range(half):
            own_cross(n).wait_send()
            relay(n).wait_send()
            for row in range(2):
                f = cross_base + n
                part_result(n, 4 - 2 * z, row, f).wait_send()
                full_copy(n, 3, row, f).wait_send()
                full_copy(n, z - 1, row, f).wait_send()
                local_copy(n, row).wait()
        for distance in range(1, 4):
            for step in range(1, peers):
                scale_copy(lax.rem(z + distance, 4), step).wait_send()

    @pl.when(z == 1)
    def _():
        for n in range(half):
            for row in range(2):
                near_copy(n, row).wait_send()

    @pl.when(z == 2)
    def _():
        for n in range(half):
            for row in range(2):
                near_local(n, row).wait()

    for hub in (1, 2):
        @pl.when(z != hub)
        def _():
            mask_copy(hub).wait_send()
            col_copy(hub).wait_send()
    for step in range(1, peers):
        part_copy(step).wait_send()
        scale_copy(z, step).wait_send()


def hub_shards(spectra, valid):
    peers = lax.axis_size("bin")
    bins, _, seg, chans = spectra.shape
    width = chans // 2
    half = bins // 2
    valid_float = valid.astype(jnp.float32)
    keep = jnp.repeat(valid_float.T, width, axis=1)
    rows = jnp.tile(valid_float, (4, 1))
    dma = pltpu.SemaphoreType.DMA
    vmem = pl.BlockSpec(memory_space=pltpu.VMEM)
    block = (2, seg, chans)
    result = (2, width, width)
    return pl.pallas_call(
        functools.partial(hub_kernel, bins * peers),
        out_shape=jax.ShapeDtypeStruct((2, 5, bins) + result, jnp.bfloat16),
        in_specs=[vmem] * 3,
        out_specs=vmem,
        scratch_shapes=[
            pltpu.VMEM((seg, chans), jnp.float32),
            pltpu.VMEM((peers - 1, seg // peers, chans), jnp.float32),
            pltpu.VMEM((4, seg, chans), jnp.float32),
            pltpu.VMEM((4, 8, seg), jnp.float32),
            pltpu.VMEM((bins,) + block, jnp.bfloat16),
            pltpu.VMEM((2, half) + block, jnp.bfloat16),
            pltpu.VMEM((4,) + block, jnp.bfloat16),
            pltpu.VMEM((half, 4, 7) + result, jnp.bfloat16),
            pltpu.VMEM((half, 4) + result, jnp.bfloat16),
            dma((bins,)), dma((bins,)), dma((half,)), dma((2, half)),
            dma((peers - 1,)), dma((peers - 1,)),
            dma((4, peers - 1)), dma((4, peers - 1)), dma((2,)), dma((4,)), dma((2,)), dma((4,)),
            dma((half, 4, 2)), dma((half, 2)), dma((bins, 2)), dma((half, 2)), dma((half, 2)),
        ],
        compiler_params=pltpu.CompilerParams(
            collective_id=0, has_side_effects=True, vmem_limit_bytes=56 * 2**20
        ),
        cost_estimate=pl.CostEstimate(
            flops=40 * bins * 2 * seg * width * width * 8, bytes_accessed=2 * spectra.size * 4,
            transcendentals=spectra.size // 2,
        ),
    )(spectra, keep, rows)


def solution(mesh):
    in_line = mesh.shape["chan"] == 4
    return jax.shard_map(
        hub_shards if in_line else shards,
        mesh=mesh,
        in_specs=(P("bin", None, None, "chan"), P("chan", None)),
        out_specs=P("chan", None, "bin", None, None, None),
        check_vma=False,
    )
```
